32 devices in a mesh: src: 8 (over y, x, core), gz: 4 (over z).
Axes of the slice: x: 2, y: 2, z: 4, core: 2. Of those that a mesh axis runs over, the one named last changes fastest.
Arguments:
- travel_times: float32 [8, 16, 128, 256], P('src', 'gz'), may hold values from -6 to 6
- upwind_codes: int32 [8, 16, 128, 256], P('src', 'gz'), may hold values from 0 to 511
- adjoint_state: float32 [8, 16, 128, 256], P('src', 'gz'), may hold values from -6 to 6
- surface_residual: float32 [8, 128, 256], P('src'), may hold values from -6 to 6
- source_cell: int32 [8], P('src'), may hold values from 0 to 524287
- slowness: float32 [16, 128, 256], P('gz'), may hold values from 0.2 to 1
Outputs:
- adjoint_next: float32 [8, 16, 128, 256], P('src', 'gz')
- coarse_kernel: float32 [8, 64, 128], P('gz')
The draws below stay inside these ranges and needn't reach their ends.
Inputs may be any that keep to these rules, and one draw needn't show every extreme that they name: `upwind_codes`: each code holds for x, y and z (bits 0 to 2, 3 to 5, 6 to 8) a low-side bit, a high-side bit and a double-weight bit; codes may name neighbours outside the grid.
All inputs are finite; a program needn't handle non-finite values.
Results may differ from the reference program's by a relative error of at most 0.0003.
Values sent between devices are 32-bit elements; how exact they have to be, the bound alone decides.
A program may use at most 128 MiB of HBM per device.

```python
import math
import jax
import jax.numpy as jnp
from jax import lax

NY = 128
NX = 256
SRC = 8
NZ = 16


def plant(values, stream_key, low, high):
    spot = [jax.random.randint(jax.random.fold_in(stream_key, axis), (), 0, length) for axis, length in enumerate(values.shape)]
    longest = values.shape.index(max(values.shape))
    neighbour = spot[:longest] + [(spot[longest] + 1) % values.shape[longest]] + spot[longest + 1:]
    return values.at[tuple(spot)].set(low).at[tuple(neighbour)].set(high)


def steps_of(key, shape, pieces, low, high):
    def one(position, shards_of):
        steps = jax.random.uniform(jax.random.fold_in(jax.random.fold_in(key, 6), position), (shards_of,), jnp.float32, low / len(pieces), high / len(pieces))
        return jnp.repeat(jnp.exp(steps), shape[position] // shards_of).reshape((-1,) + (1,) * (len(shape) - position - 1))

    gain = one(*pieces[0])
    for cut in pieces[1:]:
        gain = gain * one(*cut)
    return gain


def bell_draw(key, dims, spread, bound, pieces=(), kind=jnp.bfloat16):
    drawn = jax.random.normal(key, dims, jnp.float32) * spread
    if len(pieces) > 0:
        drawn = steps_of(key, dims, pieces, -0.22, 0.18) * drawn
    return jnp.clip(drawn, min=-bound, max=bound).astype(kind)


def setup_inputs(seed: int = 0) -> dict:
    key_list = jax.random.split(jax.random.key(seed), 7)
    return {
        "travel_times": bell_draw(key_list[0], (SRC, NZ, NY, NX), 1.0, 6.0, ((0, 8), (1, 4)), jnp.float32),
        "upwind_codes": plant(jax.random.randint(key_list[1], (SRC, NZ, NY, NX), 0, 512), jax.random.fold_in(key_list[1], 1), 0, 511).astype(jnp.int32),
        "adjoint_state": bell_draw(key_list[2], (SRC, NZ, NY, NX), 1.0, 6.0, ((0, 8), (1, 4)), jnp.float32),
        "surface_residual": bell_draw(key_list[3], (SRC, NY, NX), 1.0, 6.0, ((0, 8),), jnp.float32),
        "source_cell": plant(jax.random.randint(key_list[4], (SRC,), 0, NZ * NY * NX), jax.random.fold_in(key_list[4], 1), 0, (NZ * NY * NX) - 1).astype(jnp.int32),
        "slowness": jnp.clip(jnp.exp(math.log(1.0) - 1.609438 * jax.random.uniform(key_list[5], (NZ, NY, NX), jnp.float32) ** steps_of(key_list[5], (NZ, NY, NX), ((0, 4),), -0.2, 0.2)), 0.2, 1.0),
    }


def axis_pair(centre, low_side, high_side, code_field, low_ok, high_ok):
    used_low = (code_field % 2).astype(jnp.float32)
    used_high = ((code_field // 2) % 2).astype(jnp.float32)
    factor = 1.0 + ((code_field // 4) % 2).astype(jnp.float32)
    weight_low = factor * used_low * low_ok * jnp.abs(centre - low_side)
    weight_high = factor * used_high * high_ok * jnp.abs(centre - high_side)
    return weight_low, weight_high


def one_source(item):
    times_grid, codes_grid, adjoint, residual, cell_index, slow_grid = item
    z_index = jnp.arange(NZ).astype(jnp.int32)[:, None, None]
    y_index = jnp.arange(NY).astype(jnp.int32)[None, :, None]
    x_index = jnp.arange(NX).astype(jnp.int32)[None, None, :]
    padded_z = jnp.pad(times_grid, ((1, 1), (0, 0), (0, 0)))
    padded_y = jnp.pad(times_grid, ((0, 0), (1, 1), (0, 0)))
    padded_x = jnp.pad(times_grid, ((0, 0), (0, 0), (1, 1)))
    low_z, high_z = axis_pair(times_grid, padded_z[:-2], padded_z[2:], (codes_grid // 64) % 8,
                              (z_index >= 1).astype(jnp.float32), (z_index <= NZ - 2).astype(jnp.float32))
    low_y, high_y = axis_pair(times_grid, padded_y[:, :-2], padded_y[:, 2:], (codes_grid // 8) % 8,
                              (y_index >= 1).astype(jnp.float32), (y_index <= NY - 2).astype(jnp.float32))
    low_x, high_x = axis_pair(times_grid, padded_x[:, :, :-2], padded_x[:, :, 2:], codes_grid % 8,
                              (x_index >= 1).astype(jnp.float32), (x_index <= NX - 2).astype(jnp.float32))
    diagonal = 1.0 + low_z + high_z + low_y + high_y + low_x + high_x
    forcing = jnp.where(z_index == 0, residual[None, :, :], jnp.float32(0.0))
    flat_index = (z_index * NY + y_index) * NX + x_index
    keep_mask = flat_index != cell_index
    for sweep_index in range(2):
        incoming = jnp.pad(high_z * adjoint, ((1, 0), (0, 0), (0, 0)))[:-1]
        incoming = incoming + jnp.pad(low_z * adjoint, ((0, 1), (0, 0), (0, 0)))[1:]
        incoming = incoming + jnp.pad(high_y * adjoint, ((0, 0), (1, 0), (0, 0)))[:, :-1]
        incoming = incoming + jnp.pad(low_y * adjoint, ((0, 0), (0, 1), (0, 0)))[:, 1:]
        incoming = incoming + jnp.pad(high_x * adjoint, ((0, 0), (0, 0), (1, 0)))[:, :, :-1]
        incoming = incoming + jnp.pad(low_x * adjoint, ((0, 0), (0, 0), (0, 1)))[:, :, 1:]
        adjoint = jnp.where(keep_mask, (forcing + incoming) / diagonal, jnp.float32(0.0))
    product = adjoint * slow_grid
    coarse = product.reshape(NZ // 2, 2, NY // 2, 2, NX // 2, 2).mean(axis=(1, 3, 5))
    return adjoint, coarse


def reference(travel_times, upwind_codes, adjoint_state, surface_residual, source_cell, slowness):
    def mapped(item):
        return one_source((item[0], item[1], item[2], item[3], item[4], slowness))

    adjoint_next, coarse_all = lax.map(mapped, (travel_times, upwind_codes, adjoint_state, surface_residual, source_cell))
    return adjoint_next, jnp.sum(coarse_all, axis=0)
```

```python
import functools

import jax
import jax.numpy as jnp
from jax import lax
from jax.experimental import pallas as pl
from jax.experimental.pallas import tpu as pltpu
from jax.sharding import PartitionSpec as P

MESH = pl.DeviceIdType.MESH
CH = 32


def kernel(
    n_src, n_gz,
    t_hbm, c_hbm, a_hbm, res_hbm, cell_ref, slow_hbm,
    out_hbm, coarse_hbm,
    t, code, lam, lam1, res, slow,
    wlx, whx, wly, why, wlz, whz, diag,
    num, dface, fac, g_out, t_in, g_in,
    pool, pairs, part, rs_in, total,
    load_sem, t_send, t_recv, g_send, g_recv, rs_send, rs_recv, ag_send, ag_recv, out_sem,
):
    L, NY, NX = t.shape
    K = NY // CH
    me_s, me_z = lax.axis_index("src"), lax.axis_index("gz")
    has_lo, has_hi = me_z > 0, me_z < n_gz - 1
    layer = (0, L - 1)
    exists = (has_lo, has_hi)
    target = (me_z - 1, me_z + 1)
    f32 = jnp.float32

    barrier = pltpu.get_barrier_semaphore()
    for s in range(2):
        @pl.when(exists[s])
        def _(s=s):
            pl.semaphore_signal(barrier, 1, device_id={"gz": target[s]}, device_id_type=MESH)
    for i in range(1, n_src):
        pl.semaphore_signal(
            barrier, 1, device_id={"src": lax.rem(me_s + i, n_src)}, device_id_type=MESH
        )

    loads = {}

    def load(name, src, dst):
        copy = pltpu.make_async_copy(src, dst, load_sem.at[len(loads)])
        copy.start()
        loads[name] = copy

    order = [0, L - 1] + list(range(1, L - 1))
    for l in order[:2]:
        load(("c", l), c_hbm.at[0, l], code.at[l])
        load(("a", l), a_hbm.at[0, l], lam.at[l])
    for l in order:
        load(("t", l), t_hbm.at[0, l], t.at[l])
    for l in order[2:]:
        load(("c", l), c_hbm.at[0, l], code.at[l])
        load(("a", l), a_hbm.at[0, l], lam.at[l])
    load("res", res_hbm.at[0], res)
    for l in range(L):
        load(("s", l), slow_hbm.at[l], slow.at[l])

    def rows(k):
        return pl.ds(pl.multiple_of(k * CH, CH), CH)

    def t_copy(s, k):
        return pltpu.make_async_remote_copy(
            src_ref=t_hbm.at[0, layer[s], rows(k)], dst_ref=t_in.at[1 - s, rows(k)],
            send_sem=t_send.at[s, k], recv_sem=t_recv.at[1 - s, k],
            device_id={"gz": target[s]}, device_id_type=MESH)

    def t_arrival(s, k):
        return pltpu.make_async_remote_copy(
            src_ref=t_hbm.at[0, layer[s], rows(k)], dst_ref=t_in.at[s, rows(k)],
            send_sem=t_send.at[s, k], recv_sem=t_recv.at[s, k],
            device_id={"gz": target[s]}, device_id_type=MESH)

    def g_copy(sweep, s, k):
        return pltpu.make_async_remote_copy(
            src_ref=g_out.at[sweep, s, rows(k)], dst_ref=g_in.at[sweep, 1 - s, rows(k)],
            send_sem=g_send.at[sweep, s, k], recv_sem=g_recv.at[sweep, 1 - s, k],
            device_id={"gz": target[s]}, device_id_type=MESH)

    def g_arrival(sweep, s, k):
        return pltpu.make_async_remote_copy(
            src_ref=g_out.at[sweep, s, rows(k)], dst_ref=g_in.at[sweep, s, rows(k)],
            send_sem=g_send.at[sweep, s, k], recv_sem=g_recv.at[sweep, s, k],
            device_id={"gz": target[s]}, device_id_type=MESH)

    for s in range(2):
        @pl.when(jnp.logical_not(exists[s]))
        def _(s=s):
            t_in[s] = jnp.zeros((NY, NX), f32)
            g_in[0, s] = jnp.zeros((NY, NX), f32)
            g_in[1, s] = jnp.zeros((NY, NX), f32)

    for l in order[:2]:
        loads["c", l].wait()
        loads["a", l].wait()

    pl.semaphore_wait(
        barrier, n_src - 1 + has_lo.astype(jnp.int32) + has_hi.astype(jnp.int32)
    )

    def factors(c, shift):
        factor = jnp.where((c & (4 << shift)) != 0, f32(2.0), f32(1.0))
        low = jnp.where((c & (1 << shift)) != 0, factor, f32(0.0))
        high = jnp.where((c & (2 << shift)) != 0, factor, f32(0.0))
        return low, high

    def first_sends(k, carry):
        for s in range(2):
            @pl.when(exists[s])
            def _(s=s):
                t_copy(s, k).start()
        for s in range(2):
            f = factors(code[layer[s], rows(k)], 6)[s]
            fac[s, rows(k)] = f
            g_out[0, s, rows(k)] = f * lam[layer[s], rows(k)]
            @pl.when(exists[s])
            def _(s=s):
                g_copy(0, s, k).start()
        return carry

    lax.fori_loop(0, K, first_sends, 0)

    row_iota = lax.broadcasted_iota(jnp.int32, (CH, NX), 0)
    col = lax.broadcasted_iota(jnp.int32, (CH, NX), 1)
    cell = cell_ref[0]

    pool_row = lax.broadcasted_iota(jnp.int32, (NX, NX // 2), 0)
    pool_col = lax.broadcasted_iota(jnp.int32, (NX, NX // 2), 1)
    pool[...] = jnp.where(pool_row // 2 == pool_col, f32(0.125), f32(0.0)).astype(jnp.bfloat16)

    def before(k):
        return pl.ds(pl.multiple_of(lax.rem(k * CH + NY - 8, NY), 8), 8)

    def behind(k):
        return pl.ds(pl.multiple_of(lax.rem(k * CH + CH, NY), 8), 8)

    def from_low(prev, cur):
        return pltpu.roll(jnp.concatenate([prev, cur], axis=0), 1, 0)[8:]

    def from_high(cur, nxt):
        return pltpu.roll(jnp.concatenate([cur, nxt], axis=0), CH + 7, 0)[:CH]

    def keep_inverse(d, l, k):
        flat = (row_iota + k * CH) * NX + col
        keep = flat != cell - (me_z * L + l) * (NY * NX)
        return jnp.where(keep, 1.0 / d, f32(0.0))

    def weights(l, k):
        r = rows(k)
        row = row_iota + k * CH
        centre = t[l, r]
        c = code[l, r]
        dx = jnp.where(col == NX - 1, f32(0.0), jnp.abs(centre - pltpu.roll(centre, NX - 1, 1)))
        fl, fh = factors(c, 0)
        low, high = fl * pltpu.roll(dx, 1, 1), fh * dx
        wlx[l, r] = low
        whx[l, r] = high
        d = 1.0 + low + high
        fl, fh = factors(c, 3)
        down = jnp.abs(centre - from_low(t[l, before(k)], centre))
        up = jnp.abs(centre - from_high(centre, t[l, behind(k)]))
        low = fl * jnp.where(row == 0, f32(0.0), down)
        high = fh * jnp.where(row == NY - 1, f32(0.0), up)
        wly[l, r] = low
        why[l, r] = high
        d = d + low + high
        fl, fh = factors(c, 6)
        if l > 0:
            low = fl * jnp.abs(centre - t[l - 1, r])
            wlz[l, r] = low
            d = d + low
        if l < L - 1:
            high = fh * jnp.abs(centre - t[l + 1, r])
            whz[l, r] = high
            d = d + high
        if 0 < l < L - 1:
            d = keep_inverse(d, l, k)
        diag[l, r] = d

    top = (me_z == 0).astype(f32)

    def incoming(state, l, k):
        r, b, n = rows(k), before(k), behind(k)
        x = state[l, r]
        total_in = pltpu.roll(whx[l, r] * x, 1, 1) + pltpu.roll(wlx[l, r] * x, NX - 1, 1)
        total_in += from_low(why[l, b] * state[l, b], why[l, r] * x)
        total_in += from_high(wly[l, r] * x, wly[l, n] * state[l, n])
        if l > 0:
            total_in += whz[l - 1, r] * state[l - 1, r]
        if l < L - 1:
            total_in += wlz[l + 1, r] * state[l + 1, r]
        if l == 0:
            total_in += res[r] * top
        return total_in

    for l in order:
        loads["t", l].wait()
    for l in order[2:]:
        loads["c", l].wait()
        loads["a", l].wait()

    def all_weights(k, carry):
        for l in range(L):
            weights(l, k)
        return carry

    lax.fori_loop(0, K, all_weights, 0)
    loads["res"].wait()

    def local_sweep(state, result, k):
        for s in range(2):
            num[s, rows(k)] = incoming(state, layer[s], k)
        for l in range(1, L - 1):
            result[l, rows(k)] = incoming(state, l, k) * diag[l, rows(k)]

    def first_local(k, carry):
        local_sweep(lam, lam1, k)
        return carry

    lax.fori_loop(0, K, first_local, 0)

    def first_faces(k, carry):
        r = rows(k)
        for s in range(2):
            l = layer[s]
            @pl.when(exists[s])
            def _(s=s):
                t_arrival(s, k).wait_recv()
                g_arrival(0, s, k).wait_recv()
            d = jnp.where(exists[s], jnp.abs(t[l, r] - t_in[s, r]), f32(0.0))
            dface[s, r] = d
            f = fac[s, r]
            inverse = keep_inverse(diag[l, r] + f * d, l, k)
            diag[l, r] = inverse
            new = (num[s, r] + d * g_in[0, s, r]) * inverse
            lam1[l, r] = new
            g_out[1, s, r] = f * new
            @pl.when(exists[s])
            def _(s=s):
                g_copy(1, s, k).start()
        return carry

    lax.fori_loop(0, K, first_faces, 0)

    def second_local(k, carry):
        local_sweep(lam1, lam, k)
        return carry

    lax.fori_loop(0, K, second_local, 0)

    def out_copy(l):
        return pltpu.make_async_copy(lam.at[l], out_hbm.at[0, l], out_sem.at[l])

    for l in range(1, L - 1):
        out_copy(l).start()
    for l in range(L):
        loads["s", l].wait()

    CR = CH // 2
    CY = NY // 2
    SR = (L // 2) * CY // n_src

    def rs_copy(o):
        return pltpu.make_async_remote_copy(
            src_ref=part.at[pl.ds(pl.multiple_of(o * SR, SR), SR)], dst_ref=rs_in.at[me_s],
            send_sem=rs_send.at[o], recv_sem=rs_recv.at[me_s],
            device_id={"src": o}, device_id_type=MESH)

    def rs_arrival(j):
        return pltpu.make_async_remote_copy(
            src_ref=part.at[pl.ds(0, SR)], dst_ref=rs_in.at[j],
            send_sem=rs_send.at[j], recv_sem=rs_recv.at[j],
            device_id={"src": j}, device_id_type=MESH)

    def last_faces(k, carry):
        r = rows(k)
        for s in range(2):
            l = layer[s]
            @pl.when(exists[s])
            def _(s=s):
                g_arrival(1, s, k).wait_recv()
            lam[l, r] = (num[s, r] + dface[s, r] * g_in[1, s, r]) * diag[l, r]
        for j in range(L // 2):
            prod = lam[2 * j, r] * slow[2 * j, r] + lam[2 * j + 1, r] * slow[2 * j + 1, r]
            hi = prod.astype(jnp.bfloat16)
            lo = (prod - hi.astype(f32)).astype(jnp.bfloat16)
            pairs[j] = jnp.dot(hi, pool[...], preferred_element_type=f32) + jnp.dot(
                lo, pool[...], preferred_element_type=f32)
            first = j * CY + k * CR
            part[pl.ds(pl.multiple_of(first, CR), CR)] = (
                pairs[j, pl.ds(0, CR, stride=2)] + pairs[j, pl.ds(1, CR, stride=2)])
            for i in range(CR // SR):
                o = first // SR + i
                @pl.when(o != me_s)
                def _(o=o):
                    rs_copy(o).start()
        return carry

    lax.fori_loop(0, K, last_faces, 0)
    for s in range(2):
        out_copy(layer[s]).start()

    mine = pl.multiple_of(me_s * SR, SR)
    acc = part[pl.ds(mine, SR)]
    for i in range(1, n_src):
        j = lax.rem(me_s + i, n_src)
        rs_arrival(j).wait_recv()
        acc = acc + rs_in[j]
    total[...] = acc

    def place(o):
        return coarse_hbm.at[o * SR // CY, pl.ds(pl.multiple_of(lax.rem(o * SR, CY), SR), SR)]

    def ag_copy(i):
        o = lax.rem(me_s + i, n_src)
        return pltpu.make_async_remote_copy(
            src_ref=total, dst_ref=place(me_s),
            send_sem=ag_send.at[i], recv_sem=ag_recv.at[i],
            device_id={"src": o}, device_id_type=MESH)

    def ag_arrival(i):
        j = lax.rem(me_s + n_src - i, n_src)
        return pltpu.make_async_remote_copy(
            src_ref=total, dst_ref=place(j),
            send_sem=ag_send.at[i], recv_sem=ag_recv.at[i],
            device_id={"src": j}, device_id_type=MESH)

    for i in range(1, n_src):
        ag_copy(i).start()
    own = pltpu.make_async_copy(total, place(me_s), ag_send.at[0])
    own.start()

    def drain(k, carry):
        for s in range(2):
            @pl.when(exists[s])
            def _(s=s):
                t_copy(s, k).wait_send()
                g_copy(0, s, k).wait_send()
                g_copy(1, s, k).wait_send()
        return carry

    lax.fori_loop(0, K, drain, 0)
    for i in range(1, n_src):
        rs_copy(lax.rem(me_s + i, n_src)).wait_send()
    for l in range(L):
        out_copy(l).wait()
    own.wait()
    for i in range(1, n_src):
        ag_copy(i).wait_send()
    for i in range(1, n_src):
        ag_arrival(i).wait_recv()


def shards(n_src, n_gz, travel_times, upwind_codes, adjoint_state, surface_residual, source_cell, slowness):
    _, L, NY, NX = travel_times.shape
    K = NY // CH
    f32 = jnp.float32
    rows_total = (L // 2) * (NY // 2)
    share = rows_total // n_src
    field = pltpu.VMEM((L, NY, NX), f32)
    faces = pltpu.VMEM((2, NY, NX), f32)
    any_spec = pl.BlockSpec(memory_space=pl.ANY)
    dma = pltpu.SemaphoreType.DMA
    return pl.pallas_call(
        functools.partial(kernel, n_src, n_gz),
        out_shape=(
            jax.ShapeDtypeStruct(travel_times.shape, f32),
            jax.ShapeDtypeStruct((L // 2, NY // 2, NX // 2), f32),
        ),
        in_specs=[any_spec] * 4 + [pl.BlockSpec(memory_space=pltpu.SMEM), any_spec],
        out_specs=(any_spec, any_spec),
        scratch_shapes=[
            field, pltpu.VMEM((L, NY, NX), jnp.int32), field, field,
            pltpu.VMEM((NY, NX), f32), field,
            field, field, field, field, field, field, field,
            faces, faces, faces,
            pltpu.VMEM((2, 2, NY, NX), f32), faces, pltpu.VMEM((2, 2, NY, NX), f32),
            pltpu.VMEM((NX, NX // 2), jnp.bfloat16),
            pltpu.VMEM((L // 2, CH, NX // 2), f32),
            pltpu.VMEM((rows_total, NX // 2), f32),
            pltpu.VMEM((n_src, share, NX // 2), f32),
            pltpu.VMEM((share, NX // 2), f32),
            dma((4 * L + 1,)),
            dma((2, K)), dma((2, K)), dma((2, 2, K)), dma((2, 2, K)),
            dma((n_src,)), dma((n_src,)), dma((n_src,)), dma((n_src,)),
            dma((L,)),
        ],
        compiler_params=pltpu.CompilerParams(
            collective_id=0, has_side_effects=True, vmem_limit_bytes=48 * 1024 * 1024
        ),
    )(travel_times, upwind_codes, adjoint_state, surface_residual, source_cell, slowness)


def solution(mesh):
    in_specs = (
        P("src", "gz", None, None),
        P("src", "gz", None, None),
        P("src", "gz", None, None),
        P("src", None, None),
        P("src"),
        P("gz", None, None),
    )
    out_specs = (P("src", "gz", None, None), P("gz", None, None))
    body = functools.partial(shards, mesh.shape["src"], mesh.shape["gz"])
    return jax.shard_map(body, mesh=mesh, in_specs=in_specs, out_specs=out_specs, check_vma=False)
```

```python
import functools

import jax
import jax.numpy as jnp
from jax import lax
from jax.experimental import pallas as pl
from jax.experimental.pallas import tpu as pltpu
from jax.sharding import PartitionSpec as P

MESH = pl.DeviceIdType.MESH
CH = 32


def kernel(
    n_src, n_gz,
    t_hbm, c_hbm, a_hbm, res_hbm, cell_ref, slow_hbm,
    out, coarse,
    t, code, lam, lam1, res, slow,
    wlx, whx, wly, why, wlz, whz, diag,
    num, dface, fac, g_out, t_in, g_in,
    pool, pairs, part, pair_in, pair_sum, all_in,
    load_sem, t_send, t_recv, g_send, g_recv, pair_send, pair_recv, all_send, all_recv,
):
    L, NY, NX = t.shape
    K = NY // CH
    me_s, me_z = lax.axis_index("src"), lax.axis_index("gz")
    has_lo, has_hi = me_z > 0, me_z < n_gz - 1
    layer = (0, L - 1)
    exists = (has_lo, has_hi)
    target = (me_z - 1, me_z + 1)
    f32 = jnp.float32

    barrier = pltpu.get_barrier_semaphore()
    for s in range(2):
        @pl.when(exists[s])
        def _(s=s):
            pl.semaphore_signal(barrier, 1, device_id={"gz": target[s]}, device_id_type=MESH)
    for i in range(1, n_src):
        pl.semaphore_signal(
            barrier, 1, device_id={"src": lax.rem(me_s + i, n_src)}, device_id_type=MESH
        )

    loads = {}

    def load(name, src, dst):
        copy = pltpu.make_async_copy(src, dst, load_sem.at[len(loads)])
        copy.start()
        loads[name] = copy

    order = [0, L - 1] + list(range(1, L - 1))
    for l in order[:2]:
        load(("c", l), c_hbm.at[0, l], code.at[l])
        load(("a", l), a_hbm.at[0, l], lam.at[l])

    def rows(k):
        return pl.ds(pl.multiple_of(k * CH, CH), CH)

    def t_copy(s, k):
        return pltpu.make_async_remote_copy(
            src_ref=t_hbm.at[0, layer[s], rows(k)], dst_ref=t_in.at[1 - s, rows(k)],
            send_sem=t_send.at[s, k], recv_sem=t_recv.at[1 - s, k],
            device_id={"gz": target[s]}, device_id_type=MESH)

    def t_arrival(s, k):
        return pltpu.make_async_remote_copy(
            src_ref=t_hbm.at[0, layer[s], rows(k)], dst_ref=t_in.at[s, rows(k)],
            send_sem=t_send.at[s, k], recv_sem=t_recv.at[s, k],
            device_id={"gz": target[s]}, device_id_type=MESH)

    def g_copy(sweep, s, k):
        return pltpu.make_async_remote_copy(
            src_ref=g_out.at[sweep, s, rows(k)], dst_ref=g_in.at[sweep, 1 - s, rows(k)],
            send_sem=g_send.at[sweep, s, k], recv_sem=g_recv.at[sweep, 1 - s, k],
            device_id={"gz": target[s]}, device_id_type=MESH)

    def g_arrival(sweep, s, k):
        return pltpu.make_async_remote_copy(
            src_ref=g_out.at[sweep, s, rows(k)], dst_ref=g_in.at[sweep, s, rows(k)],
            send_sem=g_send.at[sweep, s, k], recv_sem=g_recv.at[sweep, s, k],
            device_id={"gz": target[s]}, device_id_type=MESH)

    pl.semaphore_wait(
        barrier, n_src - 1 + has_lo.astype(jnp.int32) + has_hi.astype(jnp.int32)
    )

    def send_t(k):
        for s in range(2):
            @pl.when(exists[s])
            def _(s=s):
                t_copy(s, k).start()

    AHEAD = 2
    for k in range(min(AHEAD, K)):
        send_t(k)

    for l in order:
        load(("t", l), t_hbm.at[0, l], t.at[l])
    for l in order[2:]:
        load(("c", l), c_hbm.at[0, l], code.at[l])
        load(("a", l), a_hbm.at[0, l], lam.at[l])
    load("res", res_hbm.at[0], res)
    for l in range(L):
        load(("s", l), slow_hbm.at[l], slow.at[l])

    for s in range(2):
        @pl.when(jnp.logical_not(exists[s]))
        def _(s=s):
            t_in[s] = jnp.zeros((NY, NX), f32)
            g_in[0, s] = jnp.zeros((NY, NX), f32)
            g_in[1, s] = jnp.zeros((NY, NX), f32)

    for l in order[:2]:
        loads["c", l].wait()
        loads["a", l].wait()

    def factors(c, shift):
        factor = jnp.where((c & (4 << shift)) != 0, f32(2.0), f32(1.0))
        low = jnp.where((c & (1 << shift)) != 0, factor, f32(0.0))
        high = jnp.where((c & (2 << shift)) != 0, factor, f32(0.0))
        return low, high

    def first_sends(k, carry):
        for s in range(2):
            f = factors(code[layer[s], rows(k)], 6)[s]
            fac[s, rows(k)] = f
            g_out[0, s, rows(k)] = f * lam[layer[s], rows(k)]
            @pl.when(exists[s])
            def _(s=s):
                g_copy(0, s, k).start()
        @pl.when(k + AHEAD < K)
        def _():
            send_t(k + AHEAD)
        return carry

    lax.fori_loop(0, K, first_sends, 0)

    row_iota = lax.broadcasted_iota(jnp.int32, (CH, NX), 0)
    col = lax.broadcasted_iota(jnp.int32, (CH, NX), 1)
    cell = cell_ref[0]

    pool_row = lax.broadcasted_iota(jnp.int32, (NX, NX // 2), 0)
    pool_col = lax.broadcasted_iota(jnp.int32, (NX, NX // 2), 1)
    pool[...] = jnp.where(pool_row // 2 == pool_col, f32(0.125), f32(0.0)).astype(jnp.bfloat16)

    def before(k):
        return pl.ds(pl.multiple_of(lax.rem(k * CH + NY - 8, NY), 8), 8)

    def behind(k):
        return pl.ds(pl.multiple_of(lax.rem(k * CH + CH, NY), 8), 8)

    def from_low(prev, cur):
        return pltpu.roll(jnp.concatenate([prev, cur], axis=0), 1, 0)[8:]

    def from_high(cur, nxt):
        return pltpu.roll(jnp.concatenate([cur, nxt], axis=0), CH + 7, 0)[:CH]

    def keep_inverse(d, l, k):
        flat = (row_iota + k * CH) * NX + col
        keep = flat != cell - (me_z * L + l) * (NY * NX)
        return jnp.where(keep, 1.0 / d, f32(0.0))

    def weights(l, k):
        r = rows(k)
        row = row_iota + k * CH
        centre = t[l, r]
        c = code[l, r]
        dx = jnp.where(col == NX - 1, f32(0.0), jnp.abs(centre - pltpu.roll(centre, NX - 1, 1)))
        fl, fh = factors(c, 0)
        low, high = fl * pltpu.roll(dx, 1, 1), fh * dx
        wlx[l, r] = low
        whx[l, r] = high
        d = 1.0 + low + high
        fl, fh = factors(c, 3)
        down = jnp.abs(centre - from_low(t[l, before(k)], centre))
        up = jnp.abs(centre - from_high(centre, t[l, behind(k)]))
        low = fl * jnp.where(row == 0, f32(0.0), down)
        high = fh * jnp.where(row == NY - 1, f32(0.0), up)
        wly[l, r] = low
        why[l, r] = high
        d = d + low + high
        fl, fh = factors(c, 6)
        if l > 0:
            low = fl * jnp.abs(centre - t[l - 1, r])
            wlz[l, r] = low
            d = d + low
        if l < L - 1:
            high = fh * jnp.abs(centre - t[l + 1, r])
            whz[l, r] = high
            d = d + high
        if 0 < l < L - 1:
            d = keep_inverse(d, l, k)
        diag[l, r] = d

    top = (me_z == 0).astype(f32)

    def incoming(state, l, k):
        r, b, n = rows(k), before(k), behind(k)
        x = state[l, r]
        total_in = pltpu.roll(whx[l, r] * x, 1, 1) + pltpu.roll(wlx[l, r] * x, NX - 1, 1)
        total_in += from_low(why[l, b] * state[l, b], why[l, r] * x)
        total_in += from_high(wly[l, r] * x, wly[l, n] * state[l, n])
        if l > 0:
            total_in += whz[l - 1, r] * state[l - 1, r]
        if l < L - 1:
            total_in += wlz[l + 1, r] * state[l + 1, r]
        if l == 0:
            total_in += res[r] * top
        return total_in

    for l in order:
        loads["t", l].wait()
    for l in order[2:]:
        loads["c", l].wait()
        loads["a", l].wait()

    def all_weights(k, carry):
        for l in range(L):
            weights(l, k)
        return carry

    lax.fori_loop(0, K, all_weights, 0)
    loads["res"].wait()

    def local_sweep(state, result, k):
        for s in range(2):
            num[s, rows(k)] = incoming(state, layer[s], k)
        for l in range(1, L - 1):
            result[l, rows(k)] = incoming(state, l, k) * diag[l, rows(k)]

    def first_local(k, carry):
        local_sweep(lam, lam1, k)
        return carry

    lax.fori_loop(0, K, first_local, 0)

    def first_faces(k, carry):
        r = rows(k)
        for s in range(2):
            l = layer[s]
            @pl.when(exists[s])
            def _(s=s):
                t_arrival(s, k).wait_recv()
                g_arrival(0, s, k).wait_recv()
            d = jnp.where(exists[s], jnp.abs(t[l, r] - t_in[s, r]), f32(0.0))
            dface[s, r] = d
            f = fac[s, r]
            inverse = keep_inverse(diag[l, r] + f * d, l, k)
            diag[l, r] = inverse
            new = (num[s, r] + d * g_in[0, s, r]) * inverse
            lam1[l, r] = new
            g_out[1, s, r] = f * new
            @pl.when(exists[s])
            def _(s=s):
                g_copy(1, s, k).start()
        return carry

    lax.fori_loop(0, K, first_faces, 0)

    def second_local(k, carry):
        local_sweep(lam1, out.at[0], k)
        return carry

    lax.fori_loop(0, K, second_local, 0)

    for l in range(L):
        loads["s", l].wait()

    CR = CH // 2
    HALF = (L // 2) * CR // 2
    partner = me_s + 1 - 2 * lax.rem(me_s, 2)
    mine = lax.rem(me_s, 2)

    def pair_copy(k):
        return pltpu.make_async_remote_copy(
            src_ref=part.at[k, 1 - mine], dst_ref=pair_in.at[k],
            send_sem=pair_send.at[k], recv_sem=pair_recv.at[k],
            device_id={"src": partner}, device_id_type=MESH)

    def all_copy(k, i):
        return pltpu.make_async_remote_copy(
            src_ref=pair_sum.at[k], dst_ref=all_in.at[k, me_s],
            send_sem=all_send.at[k, i], recv_sem=all_recv.at[k, me_s],
            device_id={"src": lax.rem(me_s + i, n_src)}, device_id_type=MESH)

    def all_arrival(k, i):
        j = lax.rem(me_s + i, n_src)
        return pltpu.make_async_remote_copy(
            src_ref=pair_sum.at[k], dst_ref=all_in.at[k, j],
            send_sem=all_send.at[k, i], recv_sem=all_recv.at[k, j],
            device_id={"src": j}, device_id_type=MESH)

    def share(k):
        pair_copy(k).wait_recv()
        both = part[k, mine] + pair_in[k]
        pair_sum[k] = both
        for i in range(1, n_src):
            all_copy(k, i).start()
        all_in[k, me_s] = both

    def last_faces(k, carry):
        r = rows(k)
        for s in range(2):
            l = layer[s]
            @pl.when(exists[s])
            def _(s=s):
                g_arrival(1, s, k).wait_recv()
            out[0, l, r] = (num[s, r] + dface[s, r] * g_in[1, s, r]) * diag[l, r]
        for j in range(L // 2):
            prod = out[0, 2 * j, r] * slow[2 * j, r] + out[0, 2 * j + 1, r] * slow[2 * j + 1, r]
            hi = prod.astype(jnp.bfloat16)
            lo = (prod - hi.astype(f32)).astype(jnp.bfloat16)
            pairs[j] = jnp.dot(hi, pool[...], preferred_element_type=f32) + jnp.dot(
                lo, pool[...], preferred_element_type=f32)
            sums = pairs[j, pl.ds(0, CR, stride=2)] + pairs[j, pl.ds(1, CR, stride=2)]
            for h in range(2):
                part[k, h, pl.ds(j * CR // 2, CR // 2)] = sums[h * CR // 2:(h + 1) * CR // 2]
        pair_copy(k).start()
        @pl.when(k > 0)
        def _():
            share(k - 1)
        return carry

    lax.fori_loop(0, K, last_faces, 0)
    share(K - 1)

    def drain(k, carry):
        for s in range(2):
            @pl.when(exists[s])
            def _(s=s):
                t_copy(s, k).wait_send()
                g_copy(0, s, k).wait_send()
                g_copy(1, s, k).wait_send()
        pair_copy(k).wait_send()
        for i in range(1, n_src):
            all_copy(k, i).wait_send()
        return carry

    def gather(k, carry):
        for i in range(1, n_src):
            all_arrival(k, i).wait_recv()
        for h in range(2):
            acc = all_in[k, h]
            for chip in range(1, n_src // 2):
                acc = acc + all_in[k, 2 * chip + h]
            for j in range(L // 2):
                first = pl.multiple_of(k * CR + h * CR // 2, CR // 2)
                coarse[j, pl.ds(first, CR // 2)] = acc[j * CR // 2:(j + 1) * CR // 2]
        return carry

    lax.fori_loop(0, K, gather, 0)
    lax.fori_loop(0, K, drain, 0)


def shards(n_src, n_gz, travel_times, upwind_codes, adjoint_state, surface_residual, source_cell, slowness):
    _, L, NY, NX = travel_times.shape
    K = NY // CH
    f32 = jnp.float32
    half = (L // 2) * (CH // 2) // 2
    field = pltpu.VMEM((L, NY, NX), f32)
    faces = pltpu.VMEM((2, NY, NX), f32)
    hbm_spec = pl.BlockSpec(memory_space=pltpu.HBM)
    dma = pltpu.SemaphoreType.DMA
    return pl.pallas_call(
        functools.partial(kernel, n_src, n_gz),
        out_shape=(
            jax.ShapeDtypeStruct(travel_times.shape, f32),
            jax.ShapeDtypeStruct((L // 2, NY // 2, NX // 2), f32),
        ),
        in_specs=[hbm_spec] * 4 + [pl.BlockSpec(memory_space=pltpu.SMEM), hbm_spec],
        out_specs=(pl.BlockSpec(memory_space=pltpu.VMEM),) * 2,
        scratch_shapes=[
            field, pltpu.VMEM((L, NY, NX), jnp.int32), field, field,
            pltpu.VMEM((NY, NX), f32), field,
            field, field, field, field, field, field, field,
            faces, faces, faces,
            pltpu.VMEM((2, 2, NY, NX), f32), faces, pltpu.VMEM((2, 2, NY, NX), f32),
            pltpu.VMEM((NX, NX // 2), jnp.bfloat16),
            pltpu.VMEM((L // 2, CH, NX // 2), f32),
            pltpu.VMEM((K, 2, half, NX // 2), f32),
            pltpu.VMEM((K, half, NX // 2), f32),
            pltpu.VMEM((K, half, NX // 2), f32),
            pltpu.VMEM((K, n_src, half, NX // 2), f32),
            dma((4 * L + 1,)),
            dma((2, K)), dma((2, K)), dma((2, 2, K)), dma((2, 2, K)),
            dma((K,)), dma((K,)), dma((K, n_src)), dma((K, n_src)),
        ],
        compiler_params=pltpu.CompilerParams(
            collective_id=0, has_side_effects=True, vmem_limit_bytes=48 * 1024 * 1024
        ),
    )(*[pltpu.with_memory_space_constraint(v, pltpu.HBM) for v in (travel_times, upwind_codes, adjoint_state, surface_residual)], source_cell, pltpu.with_memory_space_constraint(slowness, pltpu.HBM))


def solution(mesh):
    in_specs = (
        P("src", "gz", None, None),
        P("src", "gz", None, None),
        P("src", "gz", None, None),
        P("src", None, None),
        P("src"),
        P("gz", None, None),
    )
    out_specs = (P("src", "gz", None, None), P("gz", None, None))
    body = functools.partial(shards, mesh.shape["src"], mesh.shape["gz"])
    return jax.shard_map(body, mesh=mesh, in_specs=in_specs, out_specs=out_specs, check_vma=False)
```

```python
import functools

import jax
import jax.numpy as jnp
from jax import lax
from jax.experimental import pallas as pl
from jax.experimental.pallas import tpu as pltpu
from jax.sharding import PartitionSpec as P

MESH = pl.DeviceIdType.MESH
CH = 32


def kernel(
    n_src, n_gz,
    t_hbm, c_hbm, a_hbm, res_hbm, cell_ref, slow_hbm,
    out, coarse,
    t, code, lam, lam1, res, slow,
    wlx, whx, wly, why, wlz, whz, diag,
    num, dface, fac, g_out, t_in, g_in,
    pool, pairs, part, pair_in, pair_sum, all_in,
    load_sem, t_send, t_recv, g_send, g_recv, pair_send, pair_recv, all_send, all_recv,
):
    L, NY, NX = t.shape
    K = NY // CH
    me_s, me_z = lax.axis_index("src"), lax.axis_index("gz")
    has_lo, has_hi = me_z > 0, me_z < n_gz - 1
    layer = (0, L - 1)
    exists = (has_lo, has_hi)
    target = (me_z - 1, me_z + 1)
    f32 = jnp.float32

    barrier = pltpu.get_barrier_semaphore()
    for s in range(2):
        @pl.when(exists[s])
        def _(s=s):
            pl.semaphore_signal(barrier, 1, device_id={"gz": target[s]}, device_id_type=MESH)
    for i in range(1, n_src):
        pl.semaphore_signal(
            barrier, 1, device_id={"src": lax.rem(me_s + i, n_src)}, device_id_type=MESH
        )

    loads = {}

    def load(name, src, dst):
        copy = pltpu.make_async_copy(src, dst, load_sem.at[len(loads)])
        copy.start()
        loads[name] = copy

    order = [0, L - 1] + list(range(1, L - 1))
    for l in order[:2]:
        load(("c", l), c_hbm.at[0, l], code.at[l])
        load(("a", l), a_hbm.at[0, l], lam.at[l])

    def rows(k):
        return pl.ds(pl.multiple_of(k * CH, CH), CH)

    def t_copy(s, k):
        return pltpu.make_async_remote_copy(
            src_ref=t_hbm.at[0, layer[s], rows(k)], dst_ref=t_in.at[1 - s, rows(k)],
            send_sem=t_send.at[s], recv_sem=t_recv.at[1 - s, k],
            device_id={"gz": target[s]}, device_id_type=MESH)

    def t_arrival(s, k):
        return pltpu.make_async_remote_copy(
            src_ref=t_hbm.at[0, layer[s], rows(k)], dst_ref=t_in.at[s, rows(k)],
            send_sem=t_send.at[s], recv_sem=t_recv.at[s, k],
            device_id={"gz": target[s]}, device_id_type=MESH)

    def g_copy(sweep, s, k):
        return pltpu.make_async_remote_copy(
            src_ref=g_out.at[sweep, s, rows(k)], dst_ref=g_in.at[sweep, 1 - s, rows(k)],
            send_sem=g_send.at[sweep, s], recv_sem=g_recv.at[sweep, 1 - s, k],
            device_id={"gz": target[s]}, device_id_type=MESH)

    def g_arrival(sweep, s, k):
        return pltpu.make_async_remote_copy(
            src_ref=g_out.at[sweep, s, rows(k)], dst_ref=g_in.at[sweep, s, rows(k)],
            send_sem=g_send.at[sweep, s], recv_sem=g_recv.at[sweep, s, k],
            device_id={"gz": target[s]}, device_id_type=MESH)

    pl.semaphore_wait(
        barrier, n_src - 1 + has_lo.astype(jnp.int32) + has_hi.astype(jnp.int32)
    )

    def send_t(k):
        for s in range(2):
            @pl.when(exists[s])
            def _(s=s):
                t_copy(s, k).start()

    AHEAD = 2
    for k in range(min(AHEAD, K)):
        send_t(k)

    for l in order:
        load(("t", l), t_hbm.at[0, l], t.at[l])
    for l in order[2:]:
        load(("c", l), c_hbm.at[0, l], code.at[l])
        load(("a", l), a_hbm.at[0, l], lam.at[l])
    load("res", res_hbm.at[0], res)
    for l in range(L):
        load(("s", l), slow_hbm.at[l], slow.at[l])

    for s in range(2):
        @pl.when(jnp.logical_not(exists[s]))
        def _(s=s):
            t_in[s] = jnp.zeros((NY, NX), f32)
            g_in[0, s] = jnp.zeros((NY, NX), f32)
            g_in[1, s] = jnp.zeros((NY, NX), f32)

    for l in order[:2]:
        loads["c", l].wait()
        loads["a", l].wait()

    def factors(c, shift):
        factor = jnp.where((c & (4 << shift)) != 0, f32(2.0), f32(1.0))
        low = jnp.where((c & (1 << shift)) != 0, factor, f32(0.0))
        high = jnp.where((c & (2 << shift)) != 0, factor, f32(0.0))
        return low, high

    def first_sends(k, carry):
        for s in range(2):
            f = factors(code[layer[s], rows(k)], 6)[s]
            fac[s, rows(k)] = f
            g_out[0, s, rows(k)] = f * lam[layer[s], rows(k)]
            @pl.when(exists[s])
            def _(s=s):
                g_copy(0, s, k).start()
        @pl.when(k + AHEAD < K)
        def _():
            send_t(k + AHEAD)
        return carry

    lax.fori_loop(0, K, first_sends, 0)

    row_iota = lax.broadcasted_iota(jnp.int32, (CH, NX), 0)
    col = lax.broadcasted_iota(jnp.int32, (CH, NX), 1)
    cell = cell_ref[0]

    pool_row = lax.broadcasted_iota(jnp.int32, (NX, NX // 2), 0)
    pool_col = lax.broadcasted_iota(jnp.int32, (NX, NX // 2), 1)
    pool[...] = jnp.where(pool_row // 2 == pool_col, f32(0.125), f32(0.0)).astype(jnp.bfloat16)

    def before(k):
        return pl.ds(pl.multiple_of(lax.rem(k * CH + NY - 8, NY), 8), 8)

    def behind(k):
        return pl.ds(pl.multiple_of(lax.rem(k * CH + CH, NY), 8), 8)

    def from_low(prev, cur):
        return pltpu.roll(jnp.concatenate([prev, cur], axis=0), 1, 0)[8:]

    def from_high(cur, nxt):
        return pltpu.roll(jnp.concatenate([cur, nxt], axis=0), CH + 7, 0)[:CH]

    def keep_inverse(d, l, k):
        flat = (row_iota + k * CH) * NX + col
        keep = flat != cell - (me_z * L + l) * (NY * NX)
        return jnp.where(keep, 1.0 / d, f32(0.0))

    def weights(l, k):
        r = rows(k)
        row = row_iota + k * CH
        centre = t[l, r]
        c = code[l, r]
        dx = jnp.where(col == NX - 1, f32(0.0), jnp.abs(centre - pltpu.roll(centre, NX - 1, 1)))
        fl, fh = factors(c, 0)
        low, high = fl * pltpu.roll(dx, 1, 1), fh * dx
        wlx[l, r] = low
        whx[l, r] = high
        d = 1.0 + low + high
        fl, fh = factors(c, 3)
        down = jnp.abs(centre - from_low(t[l, before(k)], centre))
        up = jnp.abs(centre - from_high(centre, t[l, behind(k)]))
        low = fl * jnp.where(row == 0, f32(0.0), down)
        high = fh * jnp.where(row == NY - 1, f32(0.0), up)
        wly[l, r] = low
        why[l, r] = high
        d = d + low + high
        fl, fh = factors(c, 6)
        if l > 0:
            low = fl * jnp.abs(centre - t[l - 1, r])
            wlz[l, r] = low
            d = d + low
        if l < L - 1:
            high = fh * jnp.abs(centre - t[l + 1, r])
            whz[l, r] = high
            d = d + high
        if 0 < l < L - 1:
            d = keep_inverse(d, l, k)
        diag[l, r] = d

    top = (me_z == 0).astype(f32)

    def incoming(state, l, k):
        r, b, n = rows(k), before(k), behind(k)
        x = state[l, r]
        total_in = pltpu.roll(whx[l, r] * x, 1, 1) + pltpu.roll(wlx[l, r] * x, NX - 1, 1)
        total_in += from_low(why[l, b] * state[l, b], why[l, r] * x)
        total_in += from_high(wly[l, r] * x, wly[l, n] * state[l, n])
        if l > 0:
            total_in += whz[l - 1, r] * state[l - 1, r]
        if l < L - 1:
            total_in += wlz[l + 1, r] * state[l + 1, r]
        if l == 0:
            total_in += res[r] * top
        return total_in

    for l in order:
        loads["t", l].wait()
    for l in order[2:]:
        loads["c", l].wait()
        loads["a", l].wait()

    def all_weights(k, carry):
        for l in range(L):
            weights(l, k)
        return carry

    lax.fori_loop(0, K, all_weights, 0)
    loads["res"].wait()

    def local_sweep(state, result, k):
        for s in range(2):
            num[s, rows(k)] = incoming(state, layer[s], k)
        for l in range(1, L - 1):
            result[l, rows(k)] = incoming(state, l, k) * diag[l, rows(k)]

    def first_local(k, carry):
        local_sweep(lam, lam1, k)
        return carry

    lax.fori_loop(0, K, first_local, 0)

    def first_faces(k, carry):
        r = rows(k)
        for s in range(2):
            l = layer[s]
            @pl.when(exists[s])
            def _(s=s):
                t_arrival(s, k).wait_recv()
                g_arrival(0, s, k).wait_recv()
            d = jnp.where(exists[s], jnp.abs(t[l, r] - t_in[s, r]), f32(0.0))
            dface[s, r] = d
            f = fac[s, r]
            inverse = keep_inverse(diag[l, r] + f * d, l, k)
            diag[l, r] = inverse
            new = (num[s, r] + d * g_in[0, s, r]) * inverse
            lam1[l, r] = new
            g_out[1, s, r] = f * new
            @pl.when(exists[s])
            def _(s=s):
                g_copy(1, s, k).start()
        return carry

    lax.fori_loop(0, K, first_faces, 0)

    def second_local(k, carry):
        local_sweep(lam1, out.at[0], k)
        return carry

    lax.fori_loop(0, K, second_local, 0)

    for l in range(L):
        loads["s", l].wait()

    CR = CH // 2
    HALF = (L // 2) * CR // 2
    partner = me_s + 1 - 2 * lax.rem(me_s, 2)
    mine = lax.rem(me_s, 2)

    def pair_copy(k):
        return pltpu.make_async_remote_copy(
            src_ref=part.at[k, 1 - mine], dst_ref=pair_in.at[k],
            send_sem=pair_send.at[k], recv_sem=pair_recv.at[k],
            device_id={"src": partner}, device_id_type=MESH)

    def all_copy(k, i):
        return pltpu.make_async_remote_copy(
            src_ref=pair_sum.at[k], dst_ref=all_in.at[k, me_s],
            send_sem=all_send.at[k], recv_sem=all_recv.at[k],
            device_id={"src": lax.rem(me_s + i, n_src)}, device_id_type=MESH)

    def all_done(k):
        others = all_in.at[k, pl.ds(0, n_src - 1)]
        return pltpu.make_async_remote_copy(
            src_ref=others, dst_ref=others, send_sem=all_send.at[k], recv_sem=all_recv.at[k],
            device_id={"src": partner}, device_id_type=MESH)

    def share(k):
        pair_copy(k).wait_recv()
        both = part[k, mine] + pair_in[k]
        pair_sum[k] = both
        for i in range(1, n_src):
            all_copy(k, i).start()
        all_in[k, me_s] = both

    def last_faces(k, carry):
        r = rows(k)
        for s in range(2):
            l = layer[s]
            @pl.when(exists[s])
            def _(s=s):
                g_arrival(1, s, k).wait_recv()
            out[0, l, r] = (num[s, r] + dface[s, r] * g_in[1, s, r]) * diag[l, r]
        for j in range(L // 2):
            prod = out[0, 2 * j, r] * slow[2 * j, r] + out[0, 2 * j + 1, r] * slow[2 * j + 1, r]
            hi = prod.astype(jnp.bfloat16)
            lo = (prod - hi.astype(f32)).astype(jnp.bfloat16)
            pairs[j] = jnp.dot(hi, pool[...], preferred_element_type=f32) + jnp.dot(
                lo, pool[...], preferred_element_type=f32)
            sums = pairs[j, pl.ds(0, CR, stride=2)] + pairs[j, pl.ds(1, CR, stride=2)]
            part[k, j // (L // 4), pl.ds(j % (L // 4) * CR, CR)] = sums
        pair_copy(k).start()
        @pl.when(k > 0)
        def _():
            share(k - 1)
        return carry

    def drain_faces(sems, sent):
        for s in range(2):
            @pl.when(exists[s])
            def _(s=s):
                pltpu.make_async_remote_copy(
                    src_ref=sent.at[s], dst_ref=sent.at[s], send_sem=sems.at[s],
                    recv_sem=t_recv.at[s, 0], device_id={"gz": target[s]}, device_id_type=MESH,
                ).wait_send()

    drain_faces(t_send, g_out.at[0])
    drain_faces(g_send.at[0], g_out.at[0])
    lax.fori_loop(0, K, last_faces, 0)
    share(K - 1)

    def drain(k, carry):
        pair_copy(k).wait_send()
        all_done(k).wait_send()
        return carry

    def gather(k, carry):
        all_done(k).wait_recv()
        for h in range(2):
            acc = all_in[k, h]
            for chip in range(1, n_src // 2):
                acc = acc + all_in[k, 2 * chip + h]
            for j in range(L // 4):
                first = pl.multiple_of(k * CR, CR)
                coarse[h * (L // 4) + j, pl.ds(first, CR)] = acc[j * CR:(j + 1) * CR]
        return carry

    lax.fori_loop(0, K, gather, 0)
    lax.fori_loop(0, K, drain, 0)
    drain_faces(g_send.at[1], g_out.at[1])


def shards(n_src, n_gz, travel_times, upwind_codes, adjoint_state, surface_residual, source_cell, slowness):
    _, L, NY, NX = travel_times.shape
    K = NY // CH
    f32 = jnp.float32
    half = (L // 2) * (CH // 2) // 2
    field = pltpu.VMEM((L, NY, NX), f32)
    faces = pltpu.VMEM((2, NY, NX), f32)
    hbm_spec = pl.BlockSpec(memory_space=pltpu.HBM)
    dma = pltpu.SemaphoreType.DMA
    return pl.pallas_call(
        functools.partial(kernel, n_src, n_gz),
        out_shape=(
            jax.ShapeDtypeStruct(travel_times.shape, f32),
            jax.ShapeDtypeStruct((L // 2, NY // 2, NX // 2), f32),
        ),
        in_specs=[hbm_spec] * 4 + [pl.BlockSpec(memory_space=pltpu.SMEM), hbm_spec],
        out_specs=(pl.BlockSpec(memory_space=pltpu.VMEM),) * 2,
        scratch_shapes=[
            field, pltpu.VMEM((L, NY, NX), jnp.int32), field, field,
            pltpu.VMEM((NY, NX), f32), field,
            field, field, field, field, field, field, field,
            faces, faces, faces,
            pltpu.VMEM((2, 2, NY, NX), f32), faces, pltpu.VMEM((2, 2, NY, NX), f32),
            pltpu.VMEM((NX, NX // 2), jnp.bfloat16),
            pltpu.VMEM((L // 2, CH, NX // 2), f32),
            pltpu.VMEM((K, 2, half, NX // 2), f32),
            pltpu.VMEM((K, half, NX // 2), f32),
            pltpu.VMEM((K, half, NX // 2), f32),
            pltpu.VMEM((K, n_src, half, NX // 2), f32),
            dma((4 * L + 1,)),
            dma((2,)), dma((2, K)), dma((2, 2)), dma((2, 2, K)),
            dma((K,)), dma((K,)), dma((K,)), dma((K,)),
        ],
        compiler_params=pltpu.CompilerParams(
            collective_id=0, has_side_effects=True, vmem_limit_bytes=48 * 1024 * 1024
        ),
    )(*[pltpu.with_memory_space_constraint(v, pltpu.HBM) for v in (travel_times, upwind_codes, adjoint_state, surface_residual)], source_cell, pltpu.with_memory_space_constraint(slowness, pltpu.HBM))


def solution(mesh):
    in_specs = (
        P("src", "gz", None, None),
        P("src", "gz", None, None),
        P("src", "gz", None, None),
        P("src", None, None),
        P("src"),
        P("gz", None, None),
    )
    out_specs = (P("src", "gz", None, None), P("gz", None, None))
    body = functools.partial(shards, mesh.shape["src"], mesh.shape["gz"])
    return jax.shard_map(body, mesh=mesh, in_specs=in_specs, out_specs=out_specs, check_vma=False)
```
